256 devices in a mesh: dp: 64 (over y, z, core), tensor: 4 (over x).
Axes of the slice: x: 4, y: 4, z: 8, core: 2. Of those that a mesh axis runs over, the one named last changes fastest.
Arguments:
- old_weight: float32 [64, 4, 2688, 128], P('dp', 'tensor'), may hold values from -6 to 6
- old_first: float32 [64, 4, 2688, 128], P('dp', 'tensor'), may hold values from -6 to 6
- old_second: float32 [64, 4, 2688, 128], P('dp', 'tensor'), may hold values from 0.01 to 1
- gradient: bfloat16 [64, 4, 2688, 128], P('dp', 'tensor'), may hold values from -6 to 6
- old_offsets: int32 [8, 32], replicated, may hold values from 0 to 42336, as said below
- new_offsets: int32 [4, 64], replicated, may hold values from 0 to 85344, as said below
- old_heads: int32 [112], replicated, may hold values from 0 to 111, as said below
- new_heads: int32 [112], replicated, may hold values from 0 to 111, as said below
- step_count: int32 [], replicated, may hold values from 1 to 19
Outputs:
- new_weight: float32 [64, 4, 2688, 128], P('dp', 'tensor')
- new_first: float32 [64, 4, 2688, 128], P('dp', 'tensor')
- new_second: float32 [64, 4, 2688, 128], P('dp', 'tensor')
The draws below stay inside these ranges and needn't reach their ends.
Inputs may be any that keep to these rules, and one draw needn't show every extreme that they name: `old_offsets`: entry [s, 0] is 0, entries never fall along a row, entry [s, r] lies within 672 of r * 1344; a fragment holds at most 2688 units and in every row one holds exactly that many. `new_offsets`: entry [t, 0] is 0, entries never fall along a row, entry [t, i] lies within 672 of i * 1344; a fragment holds at most 2688 units and in every row one holds exactly that many. `old_heads`: each head once. Each head once; for every t and c, exactly 7 of new_heads[t * 28 : (t + 1) * 28] are among old_heads[c * 28 : (c + 1) * 28].
All inputs are finite; a program needn't handle non-finite values.
Results may differ from the reference program's by a relative error of at most 0.0003.
Values sent between devices are 32-bit elements; how exact they have to be, the bound alone decides.
No kernel may reach another device: no remote copies, remote signals or barrier semaphores. Data moves between devices by JAX's collectives and lax.ppermute only.
A program may use at most 64 MiB of HBM per device.

```python
import math
import jax
import jax.numpy as jnp

HEADS = 112
HEAD_DIM = 128
ROWS = 1024
OLD_TP = 8
OLD_DP = 32
OLD_HEADS = 14
NEW_HEADS = 28
BLOCK = 1344
CAP = 2688
N_DP = 64
N_TENSOR = 4


def jittered_starts(key, rows_count, frag_count, block_units):
    half_block = block_units // 2
    first_key, second_key = jax.random.split(key)
    jitter = jax.random.randint(first_key, (rows_count, frag_count), -half_block, half_block + 1)
    widest = jax.random.randint(second_key, (rows_count, 1), 1, frag_count - 1)
    column_ids = jnp.broadcast_to(jnp.arange(frag_count, dtype=jnp.int32)[None, :], (rows_count, frag_count))
    jitter = jnp.where(column_ids == widest, -half_block, jitter)
    jitter = jnp.where(column_ids == widest + 1, half_block, jitter)
    jitter = jnp.where(column_ids == 0, 0, jitter)
    return (column_ids * block_units + jitter).astype(jnp.int32)


def head_layout(key):
    perm_key, column_key, order_key = jax.random.split(key, 3)
    old_order = jax.random.permutation(perm_key, HEADS).astype(jnp.int32)
    per_peer = NEW_HEADS // N_TENSOR
    column_keys = jax.random.split(column_key, N_TENSOR)
    within = jax.vmap(lambda one_key: jax.random.permutation(one_key, NEW_HEADS))(column_keys).astype(jnp.int32)
    picked = within.reshape(N_TENSOR, N_TENSOR, per_peer) + (jnp.arange(N_TENSOR, dtype=jnp.int32) * NEW_HEADS)[:, None, None]
    by_target = jnp.transpose(picked, (1, 0, 2)).reshape(N_TENSOR, NEW_HEADS)
    order_keys = jax.random.split(order_key, N_TENSOR)
    shuffled = jax.vmap(lambda one_key, row_ids: jax.random.permutation(one_key, row_ids))(order_keys, by_target)
    return (old_order, old_order[shuffled.reshape(-1)].astype(jnp.int32))


def draw_old_offsets(key, part):
    key = jax.random.fold_in(key, 5)
    return jittered_starts(key, OLD_TP, OLD_DP, BLOCK)


def draw_new_offsets(key, part):
    key = jax.random.fold_in(key, 9)
    return jittered_starts(key, N_TENSOR, N_DP, BLOCK)


def draw_old_heads(key, part):
    layout = head_layout(key)
    return layout[0]


def draw_new_heads(key, part):
    layout = head_layout(key)
    return layout[1]


def block_scale(own_key, extent, cuts, least, top_value):
    loudness, own = 1.0, jax.random.fold_in(own_key, 6)
    for position, parts in cuts:
        draws = jnp.exp(jax.random.uniform(jax.random.fold_in(own, position), (parts,), jnp.float32, least / len(cuts), top_value / len(cuts)))
        loudness = loudness * jnp.repeat(draws, extent[position] // parts).reshape([-1 if axis == position else 1 for axis in range(len(extent))])
    return loudness


def centred(rng, extent, width, most, cuts=(), kind=jnp.bfloat16):
    result = jax.random.normal(rng, extent, jnp.float32) * width
    if len(cuts) > 0:
        result = block_scale(rng, extent, cuts, -0.22, 0.18) * result
    return jnp.clip(result, min=-most, max=most).astype(kind)


def setup_inputs(seed: int = 0) -> dict:
    arg_keys = jax.random.split(jax.random.key(seed), 10)
    old_weight = centred(arg_keys[0], (N_DP, N_TENSOR, CAP, HEAD_DIM), 1.0, 6.0, ((0, 64), (1, 4)), jnp.float32)
    old_first = centred(arg_keys[1], (N_DP, N_TENSOR, CAP, HEAD_DIM), 1.0, 6.0, ((0, 64), (1, 4)), jnp.float32)
    old_second = jnp.clip(jnp.exp(math.log(1.0) - 4.6051702 * jax.random.uniform(arg_keys[2], (N_DP, N_TENSOR, CAP, HEAD_DIM), jnp.float32) ** block_scale(arg_keys[2], (N_DP, N_TENSOR, CAP, HEAD_DIM), ((0, 64), (1, 4)), -0.2, 0.2)), 0.01, 1.0)
    gradient = centred(arg_keys[3], (N_DP, N_TENSOR, CAP, HEAD_DIM), 1.0, 6.0, ((0, 64), (1, 4)))
    old_offsets = draw_old_offsets(jax.random.fold_in(arg_keys[9], 71), 0)
    new_offsets = draw_new_offsets(jax.random.fold_in(arg_keys[9], 71), 0)
    old_heads = draw_old_heads(jax.random.fold_in(arg_keys[9], 71), 0)
    new_heads = draw_new_heads(jax.random.fold_in(arg_keys[9], 71), 0)
    step_count = jax.random.randint(arg_keys[8], (), 1, 20).astype(jnp.int32)
    return {"old_weight": old_weight, "old_first": old_first, "old_second": old_second, "gradient": gradient, "old_offsets": old_offsets, "new_offsets": new_offsets, "old_heads": old_heads, "new_heads": new_heads, "step_count": step_count}


beta_one = 0.9
beta_two = 0.95
learn_rate = 0.1
weight_decay = 0.1
epsilon = 1e-08

def old_units(fragments, old_offsets):
    unit_ids = jnp.arange(OLD_DP * BLOCK, dtype=jnp.int32)
    frag_ranks = jax.vmap(lambda offset_row: jnp.searchsorted(offset_row, unit_ids, side='right'))(old_offsets).astype(jnp.int32) - 1
    starts = jnp.take_along_axis(old_offsets, frag_ranks, axis=1)
    slot_ids = unit_ids[None, :] - starts
    shards = jnp.arange(OLD_TP, dtype=jnp.int32)[:, None]
    dp_rows = 2 * frag_ranks + shards % 2
    columns = jnp.broadcast_to(shards // 2, frag_ranks.shape)
    picked = fragments[dp_rows, columns, slot_ids]
    picked = picked.reshape(OLD_TP, ROWS, OLD_HEADS, 3, HEAD_DIM)
    return jnp.transpose(picked, (1, 0, 2, 3, 4)).reshape(ROWS, HEADS, 3, HEAD_DIM)

def new_fragments(whole_slab, positions, new_offsets):
    chosen = jnp.take(whole_slab, positions, axis=1)
    chosen = chosen.reshape(ROWS, N_TENSOR, NEW_HEADS * 3, HEAD_DIM)
    flat_units = jnp.transpose(chosen, (1, 0, 2, 3)).reshape(N_TENSOR, N_DP * BLOCK, HEAD_DIM)
    frag_ends = jnp.concatenate([new_offsets[:, 1:], jnp.full((N_TENSOR, 1), N_DP * BLOCK, jnp.int32)], axis=1)
    unit_ids = new_offsets.T[:, :, None] + jnp.arange(CAP, dtype=jnp.int32)[None, None, :]
    in_range = unit_ids < frag_ends.T[:, :, None]
    clipped = jnp.minimum(unit_ids, N_DP * BLOCK - 1)
    columns = jnp.arange(N_TENSOR, dtype=jnp.int32)[None, :, None]
    fragment = flat_units[columns, clipped]
    return (fragment, in_range)

def reference(old_weight, old_first, old_second, gradient, old_offsets, new_offsets, old_heads, new_heads, step_count):
    inverse = jnp.zeros((HEADS,), jnp.int32).at[old_heads].set(jnp.arange(HEADS, dtype=jnp.int32))
    positions = inverse[new_heads]
    results = []
    in_range = None
    for fragments in (old_weight, old_first, old_second):
        whole_slab = old_units(fragments, old_offsets)
        fragment, in_range = new_fragments(whole_slab, positions, new_offsets)
        results.append(fragment)
    master, first_slots, second_slots = results
    grad_float = gradient.astype(jnp.float32)
    step_float = step_count.astype(jnp.float32)
    new_first = beta_one * first_slots + (1.0 - beta_one) * grad_float
    new_second = beta_two * second_slots + (1.0 - beta_two) * grad_float * grad_float
    fix_one = 1.0 - jnp.power(jnp.float32(beta_one), step_float)
    fix_two = 1.0 - jnp.power(jnp.float32(beta_two), step_float)
    adam_ratio = new_first / fix_one / (jnp.sqrt(new_second / fix_two) + epsilon)
    new_weight = master - learn_rate * (adam_ratio + weight_decay * master)
    used_mask = in_range[..., None]
    return (jnp.where(used_mask, new_weight, 0.0), jnp.where(used_mask, new_first, 0.0), jnp.where(used_mask, new_second, 0.0))
```

```python
import functools
import jax
import jax.numpy as jnp
from jax import lax
from jax.experimental import pallas as pl
from jax.experimental.pallas import tpu as pltpu
from jax.sharding import PartitionSpec as P

beta_one = 0.9
beta_two = 0.95
learn_rate = 0.1
weight_decay = 0.1
epsilon = 1e-08

CAP = 2688
BLOCK = 1344
HALF = 672
WIDE = 680
OLD_RANKS = 32
OLD_UNITS = OLD_RANKS * BLOCK
N_DP = 64
NEW_UNITS = N_DP * BLOCK
HEADS = 112
COLUMNS = 4
GROUP = HEADS // COLUMNS
OLD_HEADS = GROUP // 2
PEER = GROUP // COLUMNS
PART = 16 * PEER * 3
LANES = 128
GROUPS = ((0,), (1,), (2,))
E_ROWS = CAP + BLOCK
CHUNK = 336

ANY = pl.BlockSpec(memory_space=pl.ANY)
VMEM = pl.BlockSpec(memory_space=pltpu.VMEM)
SMEM = pl.BlockSpec(memory_space=pltpu.SMEM)


def place():
    dp = lax.axis_index("dp")
    return dp // 2, dp % 2, lax.axis_index("tensor")


def old_start(offsets, shard, rank):
    inside = offsets[shard, jnp.minimum(rank, OLD_RANKS - 1)]
    return jnp.where(rank >= OLD_RANKS, OLD_UNITS, inside)


def aligned(start):
    return pl.multiple_of(jnp.minimum(start // 8 * 8, CAP - WIDE), 8)


def own_half_slot(rank, core, start):
    return jnp.where(
        core == 0,
        jnp.maximum(rank * BLOCK - start, 0),
        rank * BLOCK + HALF - start,
    )


def pack_kernel(count, offsets, *refs):
    sources = refs[:count]
    outs = refs[count : count + 3]
    wide, sems = refs[count + 3 :]
    rank, core, column = place()
    start = offsets[2 * column + core, rank]
    up = (rank + 1) * BLOCK - start
    firsts = (
        jnp.where(core == 0, up, 0),
        jnp.where(core == 0, 0, up),
        jnp.where(
            core == 0,
            rank * BLOCK + HALF - start,
            jnp.maximum(rank * BLOCK - start, 0),
        ),
    )
    copies = []
    for j in range(count):
        for m in range(3):
            copy = pltpu.make_async_copy(
                sources[j].at[pl.ds(aligned(firsts[m]), WIDE)],
                wide.at[j, m],
                sems.at[j, m],
            )
            copy.start()
            copies.append(copy)
    for j in range(count):
        for m in range(3):
            copies[3 * j + m].wait()
            rest = firsts[m] - aligned(firsts[m])
            outs[m][j] = wide[j, m, pl.ds(rest, HALF), :]


def pack(offsets, sources):
    count = len(sources)
    out = jax.ShapeDtypeStruct((count, HALF, LANES), jnp.float32)
    return pl.pallas_call(
        functools.partial(pack_kernel, count),
        out_shape=(out, out, out),
        in_specs=[SMEM] + [ANY] * count,
        out_specs=(VMEM, VMEM, VMEM),
        scratch_shapes=[
            pltpu.VMEM((count, 3, WIDE, LANES), jnp.float32),
            pltpu.SemaphoreType.DMA((count, 3)),
        ],
        cost_estimate=pl.CostEstimate(
            flops=0, bytes_accessed=count * 6 * HALF * LANES * 4, transcendentals=0
        ),
        name="pack",
    )(offsets, *sources)


def tables_kernel(old_heads, new_heads, after, send, recv, where, used):
    column = lax.axis_index("tensor")

    def invert(i, carry):
        where[old_heads[i]] = i
        return carry

    lax.fori_loop(0, HEADS, invert, 0)
    for s in range(COLUMNS):
        target = (column + s) % COLUMNS

        def one(b, found):
            position = where[new_heads[target * GROUP + b]] - column * GROUP
            mine = (position >= 0) & (position < GROUP)
            send[s * 8 + found] = position
            return found + jnp.where(mine, 1, 0)

        lax.fori_loop(0, GROUP, one, jnp.int32(0))
        used[s] = 0

    def slot(b, carry):
        source = where[new_heads[column * GROUP + b]] // GROUP
        shift = (column - source + COLUMNS) % COLUMNS
        found = used[shift]
        recv[shift * 8 + found] = b
        used[shift] = found + 1
        return carry

    lax.fori_loop(0, GROUP, slot, 0)


def tables(old_heads, new_heads, after):
    out = jax.ShapeDtypeStruct((8 * COLUMNS,), jnp.int32)
    return pl.pallas_call(
        tables_kernel,
        out_shape=(out, out),
        in_specs=[SMEM, SMEM, ANY],
        out_specs=(SMEM, SMEM),
        scratch_shapes=[
            pltpu.SMEM((HEADS,), jnp.int32),
            pltpu.SMEM((COLUMNS,), jnp.int32),
        ],
        cost_estimate=pl.CostEstimate(flops=0, bytes_accessed=4_000_000, transcendentals=0),
        name="tables",
    )(old_heads, new_heads, after)


def spread_kernel(count, offsets, send, *refs):
    sources = refs[:count]
    halo, other_halo, swapped = refs[count : count + 3]
    outs = refs[count + 3 : count + 7]
    held, sems = refs[count + 7 :]
    rank, core, column = place()
    shard = 2 * column + core
    start = old_start(offsets, shard, rank)
    slot = own_half_slot(rank, core, start)
    rest = slot - aligned(slot)

    def split(which):
        begin = old_start(offsets, which, rank)
        end = old_start(offsets, which, rank + 1)
        cut = jnp.where(core == 0, begin - rank * BLOCK, end - rank * BLOCK - HALF)
        return jnp.clip(cut, 0, HALF)

    cuts = (split(shard), split(shard + 1 - 2 * core))
    near = pl.multiple_of(jnp.where(core == 0, WIDE, 0), 8)
    far = pl.multiple_of(jnp.where(core == 0, 0, WIDE), 8)
    copies = []
    for j in range(count):
        copies += [
            pltpu.make_async_copy(
                sources[j].at[pl.ds(aligned(slot), WIDE)],
                held.at[j, 0, pl.ds(near, WIDE)],
                sems.at[j, 0],
            ),
            pltpu.make_async_copy(
                halo.at[j], held.at[j, 0, pl.ds(far, HALF)], sems.at[j, 1]
            ),
            pltpu.make_async_copy(
                other_halo.at[j], held.at[j, 1, pl.ds(far, HALF)], sems.at[j, 2]
            ),
            pltpu.make_async_copy(
                swapped.at[j], held.at[j, 1, pl.ds(near, HALF)], sems.at[j, 3]
            ),
        ]
    for copy in copies:
        copy.start()
    for copy in copies:
        copy.wait()
    low_rest = jnp.where(core == 0, 0, rest)
    high_rest = jnp.where(core == 0, rest, 0)
    steps = 42 * lax.broadcasted_iota(jnp.int32, (8, LANES), 0)
    for s in range(COLUMNS):

        def one(q, carry):
            head = send[s * 8 + q]
            side = head // OLD_HEADS
            mine = side == core
            lane = jnp.where(mine, 0, 1)
            unit = 3 * (head - side * OLD_HEADS)
            cut = jnp.where(mine, cuts[0], cuts[1])
            low = unit + jnp.where(mine, low_rest, 0)
            high = WIDE + unit - cut + jnp.where(mine, high_rest, 0)
            for j in range(count):
                for c in range(3):
                    for half in range(2):
                        more = half * 8 * 42 + c
                        first = held[j, lane, pl.ds(low + more, 8, stride=42), :]
                        second = held[j, lane, pl.ds(high + more, 8, stride=42), :]
                        row = pl.multiple_of(q * 48 + c * 16 + half * 8, 8)
                        outs[s][j, pl.ds(row, 8), :] = jnp.where(
                            steps < cut - unit - more, first, second
                        )
            return carry

        lax.fori_loop(0, PEER, one, 0)


def spread(offsets, send, sources, halo, other_halo, swapped):
    count = len(sources)
    out = jax.ShapeDtypeStruct((count, PART, LANES), jnp.float32)
    return pl.pallas_call(
        functools.partial(spread_kernel, count),
        out_shape=(out,) * 4,
        in_specs=[SMEM, SMEM] + [ANY] * (count + 3),
        out_specs=(VMEM,) * 4,
        scratch_shapes=[
            pltpu.VMEM((count, 2, 2 * WIDE, LANES), jnp.float32),
            pltpu.SemaphoreType.DMA((count, 4)),
        ],
        cost_estimate=pl.CostEstimate(
            flops=0, bytes_accessed=count * 6 * HALF * LANES * 4, transcendentals=0
        ),
        name="spread",
    )(offsets, send, *sources, halo, other_halo, swapped)


def collect_kernel(count, recv, *refs):
    parts = refs[:4]
    low, high = refs[4:]
    for s in range(COLUMNS):
        for q in range(PEER):
            b = recv[s * 8 + q]
            for j in range(count):
                for c in range(3):
                    row = q * 48 + c * 16
                    low[j, pl.ds(3 * b + c, 8, stride=84), :] = parts[s][j, row : row + 8, :]
                    high[j, pl.ds(3 * b + c, 8, stride=84), :] = parts[s][j, row + 8 : row + 16, :]


def collect(recv, parts):
    count = parts[0].shape[0]
    out = jax.ShapeDtypeStruct((count, HALF, LANES), jnp.float32)
    return pl.pallas_call(
        functools.partial(collect_kernel, count),
        out_shape=(out, out),
        in_specs=[SMEM] + [VMEM] * 4,
        out_specs=(VMEM, VMEM),
        cost_estimate=pl.CostEstimate(
            flops=0, bytes_accessed=count * 4 * HALF * LANES * 4, transcendentals=0
        ),
        name="collect",
    )(recv, *parts)


def update_kernel(groups, offsets, fixes, *refs):
    pieces = refs[: 4 * len(groups)]
    gradient = refs[4 * len(groups)]
    weight_out, first_out, second_out = refs[4 * len(groups) + 1 : 4 * len(groups) + 4]
    held, sems = refs[4 * len(groups) + 4 :]
    dp = lax.axis_index("dp")
    column = lax.axis_index("tensor")
    start = offsets[column, dp]
    inside = offsets[column, jnp.minimum(dp + 1, N_DP - 1)]
    end = jnp.where(dp == N_DP - 1, NEW_UNITS, inside)
    step = pl.program_id(0)

    @pl.when(step == 0)
    def _():
        copies = []
        for g, members in enumerate(groups):
            for j, which in enumerate(members):
                for k in range(4):
                    copies.append(
                        pltpu.make_async_copy(
                            pieces[4 * g + k].at[j],
                            held.at[which, pl.ds(k * HALF, HALF)],
                            sems.at[which, k],
                        )
                    )
        for copy in copies:
            copy.start()
        for copy in copies:
            copy.wait()

    begin = start - (dp * BLOCK - HALF) + step * CHUNK
    left = end - start - step * CHUNK

    @pl.when(left > 0)
    def _():
        used = lax.broadcasted_iota(jnp.int32, (CHUNK, LANES), 0) < left
        master = held[0, pl.ds(begin, CHUNK), :]
        first_slots = held[1, pl.ds(begin, CHUNK), :]
        second_slots = held[2, pl.ds(begin, CHUNK), :]
        grad = gradient[...].astype(jnp.float32)
        new_first = beta_one * first_slots + (1.0 - beta_one) * grad
        new_second = beta_two * second_slots + (1.0 - beta_two) * grad * grad
        ratio = new_first / fixes[0] / (jnp.sqrt(new_second / fixes[1]) + epsilon)
        new_weight = master - learn_rate * (ratio + weight_decay * master)
        weight_out[...] = jnp.where(used, new_weight, 0.0)
        first_out[...] = jnp.where(used, new_first, 0.0)
        second_out[...] = jnp.where(used, new_second, 0.0)

    @pl.when(left <= 0)
    def _():
        nothing = jnp.zeros((CHUNK, LANES), jnp.float32)
        weight_out[...] = nothing
        first_out[...] = nothing
        second_out[...] = nothing


def update(groups, offsets, fixes, pieces, gradient):
    out = jax.ShapeDtypeStruct((CAP, LANES), jnp.float32)
    block = pl.BlockSpec((CHUNK, LANES), lambda i: (i, 0))
    return pl.pallas_call(
        functools.partial(update_kernel, groups),
        grid=(CAP // CHUNK,),
        out_shape=(out,) * 3,
        in_specs=[SMEM, SMEM] + [ANY] * len(pieces) + [block],
        out_specs=(block,) * 3,
        scratch_shapes=[
            pltpu.VMEM((3, E_ROWS, LANES), jnp.float32),
            pltpu.SemaphoreType.DMA((3, 4)),
        ],
        compiler_params=pltpu.CompilerParams(vmem_limit_bytes=16 * 1024 * 1024),
        cost_estimate=pl.CostEstimate(
            flops=30 * CAP * LANES, bytes_accessed=7 * CAP * LANES * 4, transcendentals=0
        ),
        name="update",
    )(offsets, fixes, *pieces, gradient)


def routes():
    ranks = range(OLD_RANKS)
    above = [r for r in ranks if r + 1 < OLD_RANKS]
    below = [r for r in ranks if r > 0]
    own = [(2 * r, 2 * r + 2) for r in above] + [(2 * r + 1, 2 * r - 1) for r in below]
    other = [(2 * r + 1, 2 * r + 2) for r in above] + [(2 * r, 2 * r - 1) for r in below]
    swap = [(i, i ^ 1) for i in range(N_DP)]
    return own, other, swap


def shards(
    old_weight,
    old_first,
    old_second,
    gradient,
    old_offsets,
    new_offsets,
    old_heads,
    new_heads,
    step_count,
):
    state = (old_weight[0, 0], old_first[0, 0], old_second[0, 0])
    own_route, other_route, swap_route = routes()
    shift = [[(i, (i + s) % COLUMNS) for i in range(COLUMNS)] for s in range(COLUMNS)]
    to_next = [(i, i + 1) for i in range(N_DP - 1)]
    to_last = [(i + 1, i) for i in range(N_DP - 1)]

    moved = []
    send = recv = None
    for members in GROUPS:
        sources = [state[m] for m in members]
        own_part, other_part, swap_part = pack(old_offsets, sources)
        if send is None:
            send, recv = tables(old_heads, new_heads, own_part)
        moved.append(
            (
                sources,
                lax.ppermute(own_part, "dp", own_route),
                lax.ppermute(other_part, "dp", other_route),
                lax.ppermute(swap_part, "dp", swap_route),
            )
        )
    exchanged = []
    for sources, halo, other_halo, swapped in moved:
        parts = spread(old_offsets, send, sources, halo, other_halo, swapped)
        exchanged.append(
            [parts[0]] + [lax.ppermute(parts[s], "tensor", shift[s]) for s in (1, 2, 3)]
        )
    pieces = []
    for parts in exchanged:
        low, high = collect(recv, parts)
        pieces += [
            lax.ppermute(high, "dp", to_next),
            low,
            high,
            lax.ppermute(low, "dp", to_last),
        ]
    step_float = step_count.astype(jnp.float32)
    fixes = jnp.stack(
        [
            1.0 - jnp.power(jnp.float32(beta_one), step_float),
            1.0 - jnp.power(jnp.float32(beta_two), step_float),
        ]
    )
    outs = update(GROUPS, new_offsets, fixes, pieces, gradient[0, 0])
    return tuple(out[None, None] for out in outs)


def solution(mesh):
    spread_out = P("dp", "tensor", None, None)
    return jax.shard_map(
        shards,
        mesh=mesh,
        in_specs=(spread_out,) * 4 + (P(),) * 5,
        out_specs=(spread_out,) * 3,
        check_vma=False,
    )
```

```python
import functools
import jax
import jax.numpy as jnp
from jax import lax
from jax.experimental import pallas as pl
from jax.experimental.pallas import tpu as pltpu
from jax.sharding import PartitionSpec as P

beta_one = 0.9
beta_two = 0.95
learn_rate = 0.1
weight_decay = 0.1
epsilon = 1e-08

CAP = 2688
BLOCK = 1344
HALF = 672
WIDE = 680
OLD_RANKS = 32
OLD_UNITS = OLD_RANKS * BLOCK
N_DP = 64
NEW_UNITS = N_DP * BLOCK
HEADS = 112
COLUMNS = 4
GROUP = HEADS // COLUMNS
OLD_HEADS = GROUP // 2
PEER = GROUP // COLUMNS
PART = 16 * PEER * 3
LANES = 128
ORDER = (1, 2, 0)
E_ROWS = CAP + BLOCK
CHUNK = 672
TILE = 48
LIMIT = 12 * 1024 * 1024
FIRST_LIMIT = 62 * 1024 * 1024

HBM = pl.BlockSpec(memory_space=pltpu.HBM)
ANY = pl.BlockSpec(memory_space=pl.ANY)
VMEM = pl.BlockSpec(memory_space=pltpu.VMEM)
SMEM = pl.BlockSpec(memory_space=pltpu.SMEM)


def params():
    return pltpu.CompilerParams(vmem_limit_bytes=LIMIT)


def cost(moved):
    return pl.CostEstimate(flops=0, bytes_accessed=moved, transcendentals=0)


def place():
    dp = lax.axis_index("dp")
    return dp // 2, dp % 2, lax.axis_index("tensor")


def old_start(offsets, shard, rank):
    inside = offsets[shard, jnp.minimum(rank, OLD_RANKS - 1)]
    return jnp.where(rank >= OLD_RANKS, OLD_UNITS, inside)


def first_slots_of(offsets):
    rank, core, column = place()
    base = rank * BLOCK - offsets[2 * column + core, rank]
    up = base + BLOCK
    down = jnp.maximum(base - HALF, -HALF)
    return {
        "own": jnp.where(core == 0, up, down),
        "other": jnp.where(core == 0, down, up),
        "swap": jnp.where(core == 0, base + HALF, base),
        "keep": jnp.where(core == 0, base, base + HALF),
    }


def cut_kernel(plan, offsets, *refs):
    outs = refs[3 : 3 + len(plan)]
    wide, sems = refs[3 + len(plan) :]
    firsts = first_slots_of(offsets)
    copies = []
    for out, pieces in zip(outs, plan):
        for spot, (which, kind) in enumerate(pieces):
            begin = jnp.minimum(jnp.maximum(firsts[kind], 0) // 8 * 8, CAP - WIDE)
            begin = pl.multiple_of(begin, 8)
            n = len(copies)
            copy = pltpu.make_async_copy(
                refs[which].at[pl.ds(begin, WIDE)],
                wide.at[n, pl.ds(HALF, WIDE)],
                sems.at[n],
            )
            copy.start()
            copies.append((copy, out, spot * HALF, HALF + firsts[kind] - begin))
    for n, (copy, out, to, rest) in enumerate(copies):
        copy.wait()
        out[to : to + HALF, :] = wide[n, pl.ds(rest, HALF), :]


def cut(offsets, state, plan, limit, name):
    total = sum(len(pieces) for pieces in plan)
    return pl.pallas_call(
        functools.partial(cut_kernel, plan),
        out_shape=tuple(
            jax.ShapeDtypeStruct((len(pieces) * HALF, LANES), jnp.float32) for pieces in plan
        ),
        in_specs=[SMEM] + [HBM] * 3,
        out_specs=(VMEM,) * len(plan),
        scratch_shapes=[
            pltpu.VMEM((total, HALF + WIDE, LANES), jnp.float32),
            pltpu.SemaphoreType.DMA((total,)),
        ],
        compiler_params=pltpu.CompilerParams(vmem_limit_bytes=limit),
        cost_estimate=cost(total * 2 * HALF * LANES * 4),
        name=name,
    )(offsets, *state)


def tables_kernel(old_heads, new_heads, after, send, recv, where, used):
    column = lax.axis_index("tensor")

    def invert(i, carry):
        where[old_heads[i]] = i
        return carry

    lax.fori_loop(0, HEADS, invert, 0, unroll=8)
    for s in range(COLUMNS):
        target = (column + s) % COLUMNS

        def one(b, found):
            position = where[new_heads[target * GROUP + b]] - column * GROUP
            mine = (position >= 0) & (position < GROUP)
            send[s * 8 + found] = position
            return found + jnp.where(mine, 1, 0)

        lax.fori_loop(0, GROUP, one, jnp.int32(0), unroll=4)
        used[s] = 0

    def slot(b, carry):
        source = where[new_heads[column * GROUP + b]] // GROUP
        shift = (column - source + COLUMNS) % COLUMNS
        found = used[shift]
        recv[shift * 8 + found] = b
        used[shift] = found + 1
        return carry

    lax.fori_loop(0, GROUP, slot, 0, unroll=4)


def tables(old_heads, new_heads, after):
    out = jax.ShapeDtypeStruct((8 * COLUMNS,), jnp.int32)
    return pl.pallas_call(
        tables_kernel,
        out_shape=(out, out),
        in_specs=[SMEM, SMEM, ANY],
        out_specs=(SMEM, SMEM),
        scratch_shapes=[
            pltpu.SMEM((HEADS,), jnp.int32),
            pltpu.SMEM((COLUMNS,), jnp.int32),
        ],
        compiler_params=params(),
        cost_estimate=cost(4_000_000),
        name="tables",
    )(old_heads, new_heads, after)


def spread_kernel(turn, offsets, send, keep, halo, swapped, other_halo, *outs):
    rank, core, column = place()
    shard = 2 * column + core

    def split(which):
        begin = old_start(offsets, which, rank)
        end = old_start(offsets, which, rank + 1)
        return jnp.where(core == 0, begin - rank * BLOCK, end - rank * BLOCK - HALF)

    mine_cut = split(shard)
    other_cut = split(shard + 1 - 2 * core)
    steps = 42 * lax.broadcasted_iota(jnp.int32, (8, LANES), 0)
    low = core == 0

    def choose(first, second, rows, edge):
        return jnp.where((rows < edge) == low, second, first)

    for s in range(COLUMNS):

        def one(q, carry):
            head = send[s * 8 + q]
            side = head // OLD_HEADS
            mine = side == core
            unit = 3 * (head - side * OLD_HEADS)
            for c in range(3):
                for half in range(2):
                    begin = unit + (half * 8 * 42 + c)
                    where = pl.ds(begin, 8, stride=42)
                    rows = steps + begin
                    a = choose(keep[where, :], halo[where, :], rows, mine_cut)
                    there = pl.ds(begin + turn * HALF, 8, stride=42)
                    b = choose(swapped[there, :], other_halo[where, :], rows, other_cut)
                    row = pl.multiple_of(q * 48 + c * 16 + half * 8, 8)
                    outs[s][pl.ds(row, 8), :] = jnp.where(mine, a, b)
            return carry

        lax.fori_loop(0, PEER, one, 0, unroll=True)


def spread(turn, offsets, send, keep, halo, swapped, other_halo):
    out = jax.ShapeDtypeStruct((PART, LANES), jnp.float32)
    return pl.pallas_call(
        functools.partial(spread_kernel, turn),
        out_shape=(out,) * 4,
        in_specs=[SMEM, SMEM] + [VMEM] * 4,
        out_specs=(VMEM,) * 4,
        compiler_params=params(),
        cost_estimate=cost(6 * HALF * LANES * 4),
        name="spread",
    )(offsets, send, keep, halo, swapped, other_halo)


def collect_kernel(recv, *refs):
    parts = refs[:4]
    outer, inner = refs[4:]
    lower = lax.axis_index("dp") % 2 == 0
    for s in range(COLUMNS):
        for q in range(PEER):
            b = recv[s * 8 + q]
            for c in range(3):
                row = q * 48 + c * 16
                to = pl.ds(3 * b + c, 8, stride=84)
                low = parts[s][row : row + 8, :]
                high = parts[s][row + 8 : row + 16, :]
                outer[to, :] = jnp.where(lower, low, high)
                inner[to, :] = jnp.where(lower, high, low)


def collect(recv, parts):
    out = jax.ShapeDtypeStruct((HALF, LANES), jnp.float32)
    return pl.pallas_call(
        collect_kernel,
        out_shape=(out, out),
        in_specs=[SMEM] + [VMEM] * 4,
        out_specs=(VMEM, VMEM),
        compiler_params=params(),
        cost_estimate=cost(4 * HALF * LANES * 4),
        name="collect",
    )(recv, *parts)


def window(offsets):
    dp = lax.axis_index("dp")
    column = lax.axis_index("tensor")
    start = offsets[column, dp]
    inside = offsets[column, jnp.minimum(dp + 1, N_DP - 1)]
    end = jnp.where(dp == N_DP - 1, NEW_UNITS, inside)
    return start - (dp * BLOCK - HALF), end - start


def load_pieces(pieces, held):
    core = lax.axis_index("dp") % 2
    for k, piece in enumerate(pieces):
        spot = pl.multiple_of(jnp.where(core == 0, k, 3 - k) * HALF, 8)
        held[pl.ds(spot, HALF), :] = piece[...]


def chunked(length, compute, outs, bufs, sems):
    copies = []
    for n in range(CAP // CHUNK):
        left = length - n * CHUNK

        @pl.when(left > 0)
        def _():
            def tile(i, carry):
                row = pl.multiple_of(n * CHUNK + i * TILE, TILE)
                used = lax.broadcasted_iota(jnp.int32, (TILE, LANES), 0) < length - row
                for buf, value in zip(bufs, compute(row)):
                    buf[pl.ds(row, TILE), :] = jnp.where(used, value, 0.0)
                return carry

            lax.fori_loop(0, CHUNK // TILE, tile, 0, unroll=2)

        @pl.when(left <= 0)
        def _():
            for buf in bufs:
                buf[n * CHUNK : (n + 1) * CHUNK, :] = jnp.zeros((CHUNK, LANES), jnp.float32)

        for k, (buf, out) in enumerate(zip(bufs, outs)):
            rows = pl.ds(n * CHUNK, CHUNK)
            copy = pltpu.make_async_copy(buf.at[rows], out.at[rows], sems.at[k, n])
            copy.start()
            copies.append(copy)
    for copy in copies:
        copy.wait()


def moments_kernel(offsets, fixes, *refs):
    gradient, first_out, second_out, ratio_out = refs[8:12]
    first_held, second_held, first_buf, second_buf, sems = refs[12:]
    begin, length = window(offsets)
    load_pieces(refs[:4], first_held)
    load_pieces(refs[4:8], second_held)

    def compute(row):
        rows = pl.ds(begin + row, TILE)
        grad = gradient[pl.ds(row, TILE), :].astype(jnp.float32)
        new_first = beta_one * first_held[rows, :] + (1.0 - beta_one) * grad
        new_second = beta_two * second_held[rows, :] + (1.0 - beta_two) * grad * grad
        root = jnp.sqrt(new_second * fixes[1]) + epsilon
        ratio_out[pl.ds(row, TILE), :] = new_first * fixes[0] / root
        return new_first, new_second

    chunked(length, compute, (first_out, second_out), (first_buf, second_buf), sems)


def moments(offsets, fixes, pieces, gradient):
    out = jax.ShapeDtypeStruct((CAP, LANES), jnp.float32)
    return pl.pallas_call(
        moments_kernel,
        out_shape=(out,) * 3,
        in_specs=[SMEM, SMEM] + [VMEM] * 9,
        out_specs=(ANY, ANY, VMEM),
        scratch_shapes=[
            pltpu.VMEM((E_ROWS, LANES), jnp.float32),
            pltpu.VMEM((E_ROWS, LANES), jnp.float32),
            pltpu.VMEM((CAP, LANES), jnp.float32),
            pltpu.VMEM((CAP, LANES), jnp.float32),
            pltpu.SemaphoreType.DMA((2, CAP // CHUNK)),
        ],
        compiler_params=params(),
        cost_estimate=cost(7 * CAP * LANES * 4),
        name="moments",
    )(offsets, fixes, *pieces, gradient)


def weights_kernel(offsets, *refs):
    ratio, weight_out, held, buf, sems = refs[4:]
    begin, length = window(offsets)
    load_pieces(refs[:4], held)

    def compute(row):
        master = held[pl.ds(begin + row, TILE), :]
        return (master - learn_rate * (ratio[pl.ds(row, TILE), :] + weight_decay * master),)

    chunked(length, compute, (weight_out,), (buf,), sems)


def weights(offsets, pieces, ratio):
    return pl.pallas_call(
        weights_kernel,
        out_shape=jax.ShapeDtypeStruct((CAP, LANES), jnp.float32),
        in_specs=[SMEM] + [VMEM] * 5,
        out_specs=ANY,
        scratch_shapes=[
            pltpu.VMEM((E_ROWS, LANES), jnp.float32),
            pltpu.VMEM((CAP, LANES), jnp.float32),
            pltpu.SemaphoreType.DMA((1, CAP // CHUNK)),
        ],
        compiler_params=params(),
        cost_estimate=cost(3 * CAP * LANES * 4),
        name="weights",
    )(offsets, *pieces, ratio)


def routes():
    ranks = range(OLD_RANKS)
    above = [(r + 1) % OLD_RANKS for r in ranks]
    own = [(2 * r, 2 * above[r]) for r in ranks] + [(2 * above[r] + 1, 2 * r + 1) for r in ranks]
    other = [(2 * r + 1, 2 * above[r]) for r in ranks] + [(2 * above[r], 2 * r + 1) for r in ranks]
    swap = [(i, i ^ 1) for i in range(N_DP)]
    return own, other, swap


def shards(
    old_weight,
    old_first,
    old_second,
    gradient,
    old_offsets,
    new_offsets,
    old_heads,
    new_heads,
    step_count,
):
    state = (old_weight[0, 0], old_first[0, 0], old_second[0, 0])
    own_route, other_route, swap_route = routes()
    shift = [[(i, (i + s) % COLUMNS) for i in range(COLUMNS)] for s in range(COLUMNS)]

    f, s, w = ORDER
    swap_part, *near = cut(
        old_offsets,
        state,
        (tuple((m, "swap") for m in ORDER), ((f, "own"),), ((f, "other"),)),
        FIRST_LIMIT,
        "pack",
    )
    swapped = lax.ppermute(swap_part, "dp", swap_route)
    moved = {f: [lax.ppermute(near[0], "dp", own_route), lax.ppermute(near[1], "dp", other_route)]}
    send, recv = tables(old_heads, new_heads, near[0])
    late = cut(
        old_offsets,
        state,
        tuple(((m, kind),) for m in (s, w) for kind in ("own", "other"))
        + tuple(((m, "keep"),) for m in ORDER),
        LIMIT,
        "pack",
    )
    kept = dict(zip(ORDER, late[4:]))
    moved[s] = [lax.ppermute(late[0], "dp", own_route), lax.ppermute(late[1], "dp", other_route)]
    moved[w] = [lax.ppermute(late[2], "dp", own_route), lax.ppermute(late[3], "dp", other_route)]
    pieces = {}
    for turn, m in enumerate(ORDER):
        parts = spread(turn, old_offsets, send, kept[m], moved[m][0], swapped, moved[m][1])
        parts = [parts[0]] + [lax.ppermute(parts[k], "tensor", shift[k]) for k in (1, 2, 3)]
        outer, inner = collect(recv, parts)
        pieces[m] = [
            lax.ppermute(outer, "dp", other_route),
            outer,
            inner,
            lax.ppermute(inner, "dp", swap_route),
        ]
    step_float = step_count.astype(jnp.float32)
    fixes = jnp.stack(
        [
            1.0 / (1.0 - jnp.power(jnp.float32(beta_one), step_float)),
            1.0 / (1.0 - jnp.power(jnp.float32(beta_two), step_float)),
        ]
    )
    first, second, ratio = moments(new_offsets, fixes, pieces[1] + pieces[2], gradient[0, 0])
    weight = weights(new_offsets, pieces[0], ratio)
    return tuple(out[None, None] for out in (weight, first, second))


def solution(mesh):
    spread_out = P("dp", "tensor", None, None)
    return jax.shard_map(
        shards,
        mesh=mesh,
        in_specs=(spread_out,) * 4 + (P(),) * 5,
        out_specs=(spread_out,) * 3,
        check_vma=False,
    )
```

```python
import functools
import jax
import jax.numpy as jnp
from jax import lax
from jax.experimental import pallas as pl
from jax.experimental.pallas import tpu as pltpu
from jax.sharding import PartitionSpec as P

beta_one = 0.9
beta_two = 0.95
learn_rate = 0.1
weight_decay = 0.1
epsilon = 1e-08

CAP = 2688
BLOCK = 1344
HALF = 672
WIDE = 680
OLD_RANKS = 32
OLD_UNITS = OLD_RANKS * BLOCK
N_DP = 64
NEW_UNITS = N_DP * BLOCK
HEADS = 112
COLUMNS = 4
GROUP = HEADS // COLUMNS
OLD_HEADS = GROUP // 2
PEER = GROUP // COLUMNS
PART = 16 * PEER * 3
LANES = 128
GROUPS = ((1,), (2,), (0,))
ORDER = sum(GROUPS, ())
SWAP_FIRST = True
COST_SCALE = 1000
E_ROWS = CAP + BLOCK
CHUNK = 672
TILE = 48
LIMIT = 12 * 1024 * 1024
FIRST_LIMIT = LIMIT

HBM = pl.BlockSpec(memory_space=pltpu.HBM)
ANY = pl.BlockSpec(memory_space=pl.ANY)
VMEM = pl.BlockSpec(memory_space=pltpu.VMEM)
SMEM = pl.BlockSpec(memory_space=pltpu.SMEM)


def params():
    return pltpu.CompilerParams(vmem_limit_bytes=LIMIT)


def cost(moved):
    return pl.CostEstimate(flops=0, bytes_accessed=moved // COST_SCALE, transcendentals=0)


def place():
    dp = lax.axis_index("dp")
    return dp // 2, dp % 2, lax.axis_index("tensor")


def old_start(offsets, shard, rank):
    inside = offsets[shard, jnp.minimum(rank, OLD_RANKS - 1)]
    return jnp.where(rank >= OLD_RANKS, OLD_UNITS, inside)


def first_slots_of(offsets):
    rank, core, column = place()
    base = rank * BLOCK - offsets[2 * column + core, rank]
    up = base + BLOCK
    down = jnp.maximum(base - HALF, -HALF)
    return {
        "own": jnp.where(core == 0, up, down),
        "other": jnp.where(core == 0, down, up),
        "swap": jnp.where(core == 0, base + HALF, base),
        "keep": jnp.where(core == 0, base, base + HALF),
    }


def cut_kernel(plan, offsets, *refs):
    outs = refs[3 : 3 + len(plan)]
    wide, sems = refs[3 + len(plan) :]
    firsts = first_slots_of(offsets)
    copies = []
    for out, pieces in zip(outs, plan):
        for spot, (which, kind) in enumerate(pieces):
            begin = jnp.minimum(jnp.maximum(firsts[kind], 0) // 8 * 8, CAP - WIDE)
            begin = pl.multiple_of(begin, 8)
            n = len(copies)
            copy = pltpu.make_async_copy(
                refs[which].at[pl.ds(begin, WIDE)],
                wide.at[n, pl.ds(HALF, WIDE)],
                sems.at[n],
            )
            copy.start()
            copies.append((copy, out, spot * HALF, HALF + firsts[kind] - begin))
    for n, (copy, out, to, rest) in enumerate(copies):
        copy.wait()
        out[to : to + HALF, :] = wide[n, pl.ds(rest, HALF), :]


def cut(offsets, state, plan, limit, name):
    total = sum(len(pieces) for pieces in plan)
    return pl.pallas_call(
        functools.partial(cut_kernel, plan),
        out_shape=tuple(
            pltpu.VMEM((len(pieces) * HALF, LANES), jnp.float32) for pieces in plan
        ),
        in_specs=[SMEM] + [HBM] * 3,
        out_specs=(VMEM,) * len(plan),
        scratch_shapes=[
            pltpu.VMEM((total, HALF + WIDE, LANES), jnp.float32),
            pltpu.SemaphoreType.DMA((total,)),
        ],
        compiler_params=pltpu.CompilerParams(vmem_limit_bytes=limit),
        cost_estimate=cost(total * 2 * HALF * LANES * 4),
        name=name,
    )(offsets, *state)


def tables_kernel(old_heads, new_heads, send, recv, where, used):
    column = lax.axis_index("tensor")

    def invert(i, carry):
        where[old_heads[i]] = i
        return carry

    lax.fori_loop(0, HEADS, invert, 0, unroll=8)
    for s in range(COLUMNS):
        target = (column + s) % COLUMNS

        def one(b, found):
            position = where[new_heads[target * GROUP + b]] - column * GROUP
            mine = (position >= 0) & (position < GROUP)
            send[s * 8 + found] = position
            return found + jnp.where(mine, 1, 0)

        lax.fori_loop(0, GROUP, one, jnp.int32(0), unroll=4)
        used[s] = 0

    def slot(b, carry):
        source = where[new_heads[column * GROUP + b]] // GROUP
        shift = (column - source + COLUMNS) % COLUMNS
        found = used[shift]
        recv[shift * 8 + found] = b
        used[shift] = found + 1
        return carry

    lax.fori_loop(0, GROUP, slot, 0, unroll=4)


def tables(old_heads, new_heads):
    out = jax.ShapeDtypeStruct((8 * COLUMNS,), jnp.int32)
    return pl.pallas_call(
        tables_kernel,
        out_shape=(out, out),
        in_specs=[SMEM, SMEM],
        out_specs=(SMEM, SMEM),
        scratch_shapes=[
            pltpu.SMEM((HEADS,), jnp.int32),
            pltpu.SMEM((COLUMNS,), jnp.int32),
        ],
        compiler_params=params(),
        cost_estimate=cost(4_000_000),
        name="tables",
    )(old_heads, new_heads)


def spread_kernel(turn, count, offsets, send, keep, halo, swapped, other_halo, *outs):
    rank, core, column = place()
    shard = 2 * column + core

    def split(which):
        begin = old_start(offsets, which, rank)
        end = old_start(offsets, which, rank + 1)
        return jnp.where(core == 0, begin - rank * BLOCK, end - rank * BLOCK - HALF)

    mine_cut = split(shard)
    other_cut = split(shard + 1 - 2 * core)
    steps = 42 * lax.broadcasted_iota(jnp.int32, (8, LANES), 0)
    low = core == 0

    def choose(first, second, rows, edge):
        return jnp.where((rows < edge) == low, second, first)

    for s in range(COLUMNS):

        def one(q, carry):
            head = send[s * 8 + q]
            side = head // OLD_HEADS
            mine = side == core
            unit = 3 * (head - side * OLD_HEADS)
            for j in range(count):
                for c in range(3):
                    for half in range(2):
                        begin = unit + (half * 8 * 42 + c)
                        here = pl.ds(begin + j * HALF, 8, stride=42)
                        there = pl.ds(begin + (turn + j) * HALF, 8, stride=42)
                        rows = steps + begin
                        a = choose(keep[here, :], halo[here, :], rows, mine_cut)
                        b = choose(swapped[there, :], other_halo[here, :], rows, other_cut)
                        row = pl.multiple_of(j * PART + q * 48 + c * 16 + half * 8, 8)
                        outs[s][pl.ds(row, 8), :] = jnp.where(mine, a, b)
            return carry

        lax.fori_loop(0, PEER, one, 0, unroll=True)


def spread(turn, offsets, send, keep, halo, swapped, other_halo):
    count = keep.shape[0] // HALF
    out = pltpu.VMEM((count * PART, LANES), jnp.float32)
    return pl.pallas_call(
        functools.partial(spread_kernel, turn, count),
        out_shape=(out,) * 4,
        in_specs=[SMEM, SMEM] + [VMEM] * 4,
        out_specs=(VMEM,) * 4,
        compiler_params=params(),
        cost_estimate=cost(count * 6 * HALF * LANES * 4),
        name="spread",
    )(offsets, send, keep, halo, swapped, other_halo)


def collect_kernel(count, recv, *refs):
    parts = refs[:4]
    outer, inner = refs[4:]
    lower = lax.axis_index("dp") % 2 == 0
    for s in range(COLUMNS):
        for q in range(PEER):
            b = recv[s * 8 + q]
            for j in range(count):
                for c in range(3):
                    row = j * PART + q * 48 + c * 16
                    to = pl.ds(j * HALF + 3 * b + c, 8, stride=84)
                    low = parts[s][row : row + 8, :]
                    high = parts[s][row + 8 : row + 16, :]
                    outer[to, :] = jnp.where(lower, low, high)
                    inner[to, :] = jnp.where(lower, high, low)


def collect(recv, parts):
    count = parts[0].shape[0] // PART
    out = pltpu.VMEM((count * HALF, LANES), jnp.float32)
    return pl.pallas_call(
        functools.partial(collect_kernel, count),
        out_shape=(out, out),
        in_specs=[SMEM] + [VMEM] * 4,
        out_specs=(VMEM, VMEM),
        compiler_params=params(),
        cost_estimate=cost(count * 4 * HALF * LANES * 4),
        name="collect",
    )(recv, *parts)


def window(offsets):
    dp = lax.axis_index("dp")
    column = lax.axis_index("tensor")
    start = offsets[column, dp]
    inside = offsets[column, jnp.minimum(dp + 1, N_DP - 1)]
    end = jnp.where(dp == N_DP - 1, NEW_UNITS, inside)
    return start - (dp * BLOCK - HALF), end - start


def load_pieces(pieces, turn, held):
    core = lax.axis_index("dp") % 2
    for k, piece in enumerate(pieces):
        spot = pl.multiple_of(jnp.where(core == 0, k, 3 - k) * HALF, 8)
        held[pl.ds(spot, HALF), :] = piece[turn * HALF : (turn + 1) * HALF, :]


def chunked(length, compute, outs, bufs, sems):
    copies = []
    for n in range(CAP // CHUNK):
        left = length - n * CHUNK

        @pl.when(left > 0)
        def _():
            def tile(i, carry):
                row = pl.multiple_of(n * CHUNK + i * TILE, TILE)
                used = lax.broadcasted_iota(jnp.int32, (TILE, LANES), 0) < length - row
                for buf, value in zip(bufs, compute(row)):
                    buf[pl.ds(row, TILE), :] = jnp.where(used, value, 0.0)
                return carry

            lax.fori_loop(0, CHUNK // TILE, tile, 0, unroll=2)

        @pl.when(left <= 0)
        def _():
            for buf in bufs:
                buf[n * CHUNK : (n + 1) * CHUNK, :] = jnp.zeros((CHUNK, LANES), jnp.float32)

        for k, (buf, out) in enumerate(zip(bufs, outs)):
            rows = pl.ds(n * CHUNK, CHUNK)
            copy = pltpu.make_async_copy(buf.at[rows], out.at[rows], sems.at[k, n])
            copy.start()
            copies.append(copy)
    for copy in copies:
        copy.wait()


def moments_kernel(turns, offsets, fixes, *refs):
    gradient, first_out, second_out, ratio_out = refs[8:12]
    first_held, second_held, first_buf, second_buf, sems = refs[12:]
    begin, length = window(offsets)
    load_pieces(refs[:4], turns[0], first_held)
    load_pieces(refs[4:8], turns[1], second_held)

    def compute(row):
        rows = pl.ds(begin + row, TILE)
        grad = gradient[pl.ds(row, TILE), :].astype(jnp.float32)
        new_first = beta_one * first_held[rows, :] + (1.0 - beta_one) * grad
        new_second = beta_two * second_held[rows, :] + (1.0 - beta_two) * grad * grad
        root = jnp.sqrt(new_second * fixes[1]) + epsilon
        ratio_out[pl.ds(row, TILE), :] = new_first * fixes[0] / root
        return new_first, new_second

    chunked(length, compute, (first_out, second_out), (first_buf, second_buf), sems)


def moments(turns, offsets, fixes, pieces, gradient):
    out = jax.ShapeDtypeStruct((CAP, LANES), jnp.float32)
    return pl.pallas_call(
        functools.partial(moments_kernel, turns),
        out_shape=(out,) * 3,
        in_specs=[SMEM, SMEM] + [VMEM] * 9,
        out_specs=(ANY, ANY, VMEM),
        scratch_shapes=[
            pltpu.VMEM((E_ROWS, LANES), jnp.float32),
            pltpu.VMEM((E_ROWS, LANES), jnp.float32),
            pltpu.VMEM((CAP, LANES), jnp.float32),
            pltpu.VMEM((CAP, LANES), jnp.float32),
            pltpu.SemaphoreType.DMA((2, CAP // CHUNK)),
        ],
        compiler_params=params(),
        cost_estimate=cost(7 * CAP * LANES * 4),
        name="moments",
    )(offsets, fixes, *pieces, gradient)


def weights_kernel(turn, offsets, *refs):
    ratio, weight_out, held, buf, sems = refs[4:]
    begin, length = window(offsets)
    load_pieces(refs[:4], turn, held)

    def compute(row):
        master = held[pl.ds(begin + row, TILE), :]
        return (master - learn_rate * (ratio[pl.ds(row, TILE), :] + weight_decay * master),)

    chunked(length, compute, (weight_out,), (buf,), sems)


def weights(turn, offsets, pieces, ratio):
    return pl.pallas_call(
        functools.partial(weights_kernel, turn),
        out_shape=jax.ShapeDtypeStruct((CAP, LANES), jnp.float32),
        in_specs=[SMEM] + [VMEM] * 5,
        out_specs=ANY,
        scratch_shapes=[
            pltpu.VMEM((E_ROWS, LANES), jnp.float32),
            pltpu.VMEM((CAP, LANES), jnp.float32),
            pltpu.SemaphoreType.DMA((1, CAP // CHUNK)),
        ],
        compiler_params=params(),
        cost_estimate=cost(3 * CAP * LANES * 4),
        name="weights",
    )(offsets, *pieces, ratio)


def routes():
    ranks = range(OLD_RANKS)
    above = [(r + 1) % OLD_RANKS for r in ranks]
    own = [(2 * r, 2 * above[r]) for r in ranks] + [(2 * above[r] + 1, 2 * r + 1) for r in ranks]
    other = [(2 * r + 1, 2 * above[r]) for r in ranks] + [(2 * above[r], 2 * r + 1) for r in ranks]
    swap = [(i, i ^ 1) for i in range(N_DP)]
    return own, other, swap


def shards(
    old_weight,
    old_first,
    old_second,
    gradient,
    old_offsets,
    new_offsets,
    old_heads,
    new_heads,
    step_count,
):
    state = tuple(
        pltpu.with_memory_space_constraint(member[0, 0], pltpu.HBM)
        for member in (old_weight, old_first, old_second)
    )
    own_route, other_route, swap_route = routes()
    shift = [[(i, (i + s) % COLUMNS) for i in range(COLUMNS)] for s in range(COLUMNS)]

    def halos(groups):
        return [tuple((m, kind) for m in g) for g in groups for kind in ("own", "other")]

    swap_plan = [tuple((m, "swap") for m in ORDER)]
    plan = (swap_plan if SWAP_FIRST else []) + halos(GROUPS[:1])
    rest = ([] if SWAP_FIRST else swap_plan) + halos(GROUPS[1:])
    rest += [tuple((m, "keep") for m in g) for g in GROUPS]
    near = list(cut(old_offsets, state, plan, FIRST_LIMIT, "pack"))
    near[0], later_offsets, old_heads = lax.optimization_barrier((near[0], old_offsets, old_heads))
    send, recv = tables(old_heads, new_heads)
    far = list(cut(later_offsets, state, rest, LIMIT, "pack"))
    swapped = lax.ppermute((near if SWAP_FIRST else far).pop(0), "dp", swap_route)
    halves = near + far
    moved = [
        (
            lax.ppermute(halves[2 * g], "dp", own_route),
            lax.ppermute(halves[2 * g + 1], "dp", other_route),
        )
        for g in range(len(GROUPS))
    ]
    kept = halves[2 * len(GROUPS) :]
    pieces, turns = {}, {}
    for g, members in enumerate(GROUPS):
        turn = ORDER.index(members[0])
        parts = spread(turn, old_offsets, send, kept[g], moved[g][0], swapped, moved[g][1])
        parts = [parts[0]] + [lax.ppermute(parts[k], "tensor", shift[k]) for k in (1, 2, 3)]
        outer, inner = collect(recv, parts)
        arrived = [
            lax.ppermute(outer, "dp", other_route),
            outer,
            inner,
            lax.ppermute(inner, "dp", swap_route),
        ]
        for turn, m in enumerate(members):
            pieces[m], turns[m] = arrived, turn
    step_float = step_count.astype(jnp.float32)
    fixes = jnp.stack(
        [
            1.0 / (1.0 - jnp.power(jnp.float32(beta_one), step_float)),
            1.0 / (1.0 - jnp.power(jnp.float32(beta_two), step_float)),
        ]
    )
    first, second, ratio = moments(
        (turns[1], turns[2]), new_offsets, fixes, pieces[1] + pieces[2], gradient[0, 0]
    )
    weight = weights(turns[0], new_offsets, pieces[0], ratio)
    return tuple(out[None, None] for out in (weight, first, second))


def solution(mesh):
    spread_out = P("dp", "tensor", None, None)
    return jax.shard_map(
        shards,
        mesh=mesh,
        in_specs=(spread_out,) * 4 + (P(),) * 5,
        out_specs=(spread_out,) * 3,
        check_vma=False,
    )
```

```python
import functools
import jax
import jax.numpy as jnp
from jax import lax
from jax.experimental import pallas as pl
from jax.experimental.pallas import tpu as pltpu
from jax.sharding import PartitionSpec as P

beta_one = 0.9
beta_two = 0.95
learn_rate = 0.1
weight_decay = 0.1
epsilon = 1e-08

CAP = 2688
BLOCK = 1344
HALF = 672
WIDE = 680
OLD_RANKS = 32
OLD_UNITS = OLD_RANKS * BLOCK
N_DP = 64
NEW_UNITS = N_DP * BLOCK
HEADS = 112
COLUMNS = 4
GROUP = HEADS // COLUMNS
OLD_HEADS = GROUP // 2
PEER = GROUP // COLUMNS
PART = 16 * PEER * 3
LANES = 128
GROUPS = ((1,), (2,), (0,))
ORDER = sum(GROUPS, ())
SWAP_FIRST = True
COST_SCALE = 1000
E_ROWS = CAP + BLOCK
CHUNK = 672
TILE = 48
LIMIT = 12 * 1024 * 1024
FIRST_LIMIT = LIMIT

HBM = pl.BlockSpec(memory_space=pltpu.HBM)
ANY = pl.BlockSpec(memory_space=pl.ANY)
VMEM = pl.BlockSpec(memory_space=pltpu.VMEM)
SMEM = pl.BlockSpec(memory_space=pltpu.SMEM)


def params():
    return pltpu.CompilerParams(vmem_limit_bytes=LIMIT)


def cost(moved):
    return pl.CostEstimate(flops=0, bytes_accessed=moved // COST_SCALE, transcendentals=0)


def pinned(arrays):
    return [pltpu.with_memory_space_constraint(x, pltpu.VMEM) for x in arrays]


def place():
    dp = lax.axis_index("dp")
    return dp // 2, dp % 2, lax.axis_index("tensor")


def old_start(offsets, shard, rank):
    inside = offsets[shard, jnp.minimum(rank, OLD_RANKS - 1)]
    return jnp.where(rank >= OLD_RANKS, OLD_UNITS, inside)


def first_slots_of(offsets):
    rank, core, column = place()
    base = rank * BLOCK - offsets[2 * column + core, rank]
    up = base + BLOCK
    down = jnp.maximum(base - HALF, -HALF)
    return {
        "own": jnp.where(core == 0, up, down),
        "other": jnp.where(core == 0, down, up),
        "swap": jnp.where(core == 0, base + HALF, base),
        "keep": jnp.where(core == 0, base, base + HALF),
    }


def correction(beta, steps):
    power = lax.fori_loop(0, steps[0], lambda _, value: value * beta, jnp.float32(1.0))
    return 1.0 / (1.0 - jnp.full((8, LANES), power, jnp.float32))


def first_cut_kernel(plan, offsets, steps, *refs):
    fixes = refs[3 + len(plan)]

    def meanwhile():
        fixes[0:8, :] = correction(beta_one, steps)
        fixes[8:16, :] = correction(beta_two, steps)

    cut_kernel(plan, offsets, *refs[: 3 + len(plan)], *refs[4 + len(plan) :], meanwhile=meanwhile)


def cut_kernel(plan, offsets, *refs, meanwhile=None):
    outs = refs[3 : 3 + len(plan)]
    wide, sems = refs[3 + len(plan) :]
    firsts = first_slots_of(offsets)
    copies = []
    for out, pieces in zip(outs, plan):
        for spot, (which, kind) in enumerate(pieces):
            begin = jnp.minimum(jnp.maximum(firsts[kind], 0) // 8 * 8, CAP - WIDE)
            begin = pl.multiple_of(begin, 8)
            n = len(copies)
            copy = pltpu.make_async_copy(
                refs[which].at[pl.ds(begin, WIDE)],
                wide.at[n, pl.ds(HALF, WIDE)],
                sems.at[n],
            )
            copy.start()
            copies.append((copy, out, spot * HALF, HALF + firsts[kind] - begin))
    if meanwhile is not None:
        meanwhile()
    for n, (copy, out, to, rest) in enumerate(copies):
        copy.wait()
        out[to : to + HALF, :] = wide[n, pl.ds(rest, HALF), :]


def cut(offsets, state, plan, limit, steps=None):
    total = sum(len(pieces) for pieces in plan)
    scalars = [offsets] if steps is None else [offsets, steps]
    rows = [len(pieces) * HALF for pieces in plan] + [16] * (len(scalars) - 1)
    return pl.pallas_call(
        functools.partial(cut_kernel if steps is None else first_cut_kernel, plan),
        out_shape=tuple(pltpu.VMEM((count, LANES), jnp.float32) for count in rows),
        in_specs=[SMEM] * len(scalars) + [HBM] * 3,
        out_specs=(VMEM,) * len(rows),
        scratch_shapes=[
            pltpu.VMEM((total, HALF + WIDE, LANES), jnp.float32),
            pltpu.SemaphoreType.DMA((total,)),
        ],
        compiler_params=pltpu.CompilerParams(vmem_limit_bytes=limit),
        cost_estimate=cost(total * 2 * HALF * LANES * 4),
        name="pack",
    )(*scalars, *state)


def tables_kernel(old_heads, new_heads, send, recv, where):
    column = lax.axis_index("tensor")
    for i in range(0, HEADS, GROUP):
        heads = [old_heads[i + b] for b in range(GROUP)]
        for b in range(GROUP):
            where[heads[b]] = i + b

    def spots(target):
        heads = [new_heads[target * GROUP + b] for b in range(GROUP)]
        return [where[head] for head in heads]

    for s in range(COLUMNS):
        found = jnp.int32(s * 8)
        for spot in spots((column + s) % COLUMNS):
            position = spot - column * GROUP
            send[found] = position
            found += jnp.where((position >= 0) & (position < GROUP), 1, 0)
    mine = spots(column)
    for s in range(COLUMNS):
        begin = (column + COLUMNS - s) % COLUMNS * GROUP
        found = jnp.int32(s * 8)
        for b in range(GROUP):
            recv[found] = b
            found += jnp.where((mine[b] >= begin) & (mine[b] < begin + GROUP), 1, 0)


def tables(old_heads, new_heads):
    out = jax.ShapeDtypeStruct((8 * COLUMNS,), jnp.int32)
    return pl.pallas_call(
        tables_kernel,
        out_shape=(out, out),
        in_specs=[SMEM, SMEM],
        out_specs=(SMEM, SMEM),
        scratch_shapes=[pltpu.SMEM((HEADS,), jnp.int32)],
        compiler_params=params(),
        cost_estimate=cost(4_000_000),
        name="tables",
    )(old_heads, new_heads)


def spread_kernel(turn, count, offsets, send, keep, halo, swapped, other_halo, *outs):
    rank, core, column = place()
    shard = 2 * column + core

    def split(which):
        begin = old_start(offsets, which, rank)
        end = old_start(offsets, which, rank + 1)
        return jnp.where(core == 0, begin - rank * BLOCK, end - rank * BLOCK - HALF)

    mine_cut = split(shard)
    other_cut = split(shard + 1 - 2 * core)
    steps = 42 * lax.broadcasted_iota(jnp.int32, (8, LANES), 0)
    low = core == 0

    def choose(first, second, rows, edge):
        return jnp.where((rows < edge) == low, second, first)

    for s in range(COLUMNS):

        def one(q, carry):
            head = send[s * 8 + q]
            side = head // OLD_HEADS
            mine = side == core
            unit = 3 * (head - side * OLD_HEADS)
            for j in range(count):
                for c in range(3):
                    for half in range(2):
                        begin = unit + (half * 8 * 42 + c)
                        here = pl.ds(begin + j * HALF, 8, stride=42)
                        there = pl.ds(begin + (turn + j) * HALF, 8, stride=42)
                        rows = steps + begin
                        a = choose(keep[here, :], halo[here, :], rows, mine_cut)
                        b = choose(swapped[there, :], other_halo[here, :], rows, other_cut)
                        row = pl.multiple_of(j * PART + q * 48 + c * 16 + half * 8, 8)
                        outs[s][pl.ds(row, 8), :] = jnp.where(mine, a, b)
            return carry

        lax.fori_loop(0, PEER, one, 0, unroll=True)


def spread(turn, offsets, send, keep, halo, swapped, other_halo):
    count = keep.shape[0] // HALF
    out = pltpu.VMEM((count * PART, LANES), jnp.float32)
    return pl.pallas_call(
        functools.partial(spread_kernel, turn, count),
        out_shape=(out,) * 4,
        in_specs=[SMEM, SMEM] + [VMEM] * 4,
        out_specs=(VMEM,) * 4,
        compiler_params=params(),
        cost_estimate=cost(count * 6 * HALF * LANES * 4),
        name="spread",
    )(offsets, send, *pinned([keep, halo, swapped, other_halo]))


def collect_kernel(count, recv, *refs):
    parts = refs[:4]
    outer, inner = refs[4:]
    lower = lax.axis_index("dp") % 2 == 0
    for s in range(COLUMNS):
        for q in range(PEER):
            b = recv[s * 8 + q]
            for j in range(count):
                for c in range(3):
                    row = j * PART + q * 48 + c * 16
                    to = pl.ds(j * HALF + 3 * b + c, 8, stride=84)
                    low = parts[s][row : row + 8, :]
                    high = parts[s][row + 8 : row + 16, :]
                    outer[to, :] = jnp.where(lower, low, high)
                    inner[to, :] = jnp.where(lower, high, low)


def collect(recv, parts):
    count = parts[0].shape[0] // PART
    out = pltpu.VMEM((count * HALF, LANES), jnp.float32)
    return pl.pallas_call(
        functools.partial(collect_kernel, count),
        out_shape=(out, out),
        in_specs=[SMEM] + [VMEM] * 4,
        out_specs=(VMEM, VMEM),
        compiler_params=params(),
        cost_estimate=cost(count * 4 * HALF * LANES * 4),
        name="collect",
    )(recv, *pinned(parts))


def window(offsets):
    dp = lax.axis_index("dp")
    column = lax.axis_index("tensor")
    start = offsets[column, dp]
    inside = offsets[column, jnp.minimum(dp + 1, N_DP - 1)]
    end = jnp.where(dp == N_DP - 1, NEW_UNITS, inside)
    return start - (dp * BLOCK - HALF), end - start


def load_pieces(pieces, turn, held):
    core = lax.axis_index("dp") % 2
    for k, piece in enumerate(pieces):
        spot = pl.multiple_of(jnp.where(core == 0, k, 3 - k) * HALF, 8)
        held[pl.ds(spot, HALF), :] = piece[turn * HALF : (turn + 1) * HALF, :]


def chunked(length, compute, outs, bufs, sems):
    copies = []
    for n in range(CAP // CHUNK):
        left = length - n * CHUNK

        @pl.when(left > 0)
        def _():
            def tile(i, carry):
                row = pl.multiple_of(n * CHUNK + i * TILE, TILE)
                used = lax.broadcasted_iota(jnp.int32, (TILE, LANES), 0) < length - row
                for buf, value in zip(bufs, compute(row)):
                    buf[pl.ds(row, TILE), :] = jnp.where(used, value, 0.0)
                return carry

            lax.fori_loop(0, CHUNK // TILE, tile, 0, unroll=2)

        @pl.when(left <= 0)
        def _():
            for buf in bufs:
                buf[n * CHUNK : (n + 1) * CHUNK, :] = jnp.zeros((CHUNK, LANES), jnp.float32)

        for k, (buf, out) in enumerate(zip(bufs, outs)):
            rows = pl.ds(n * CHUNK, CHUNK)
            copy = pltpu.make_async_copy(buf.at[rows], out.at[rows], sems.at[k, n])
            copy.start()
            copies.append(copy)
    for copy in copies:
        copy.wait()


def moments_kernel(turns, offsets, *refs):
    fixes, gradient, first_out, second_out, ratio_out = refs[8:13]
    first_held, second_held, first_buf, second_buf, sems = refs[13:]
    begin, length = window(offsets)
    load_pieces(refs[:4], turns[0], first_held)
    load_pieces(refs[4:8], turns[1], second_held)

    fix_one, fix_two = fixes[0:1, :], fixes[8:9, :]

    def compute(row):
        rows = pl.ds(begin + row, TILE)
        grad = gradient[pl.ds(row, TILE), :].astype(jnp.float32)
        new_first = beta_one * first_held[rows, :] + (1.0 - beta_one) * grad
        new_second = beta_two * second_held[rows, :] + (1.0 - beta_two) * grad * grad
        root = jnp.sqrt(new_second * fix_two) + epsilon
        ratio_out[pl.ds(row, TILE), :] = new_first * fix_one / root
        return new_first, new_second

    chunked(length, compute, (first_out, second_out), (first_buf, second_buf), sems)


def moments(turns, offsets, fixes, pieces, gradient):
    out = jax.ShapeDtypeStruct((CAP, LANES), jnp.float32)
    return pl.pallas_call(
        functools.partial(moments_kernel, turns),
        out_shape=(out,) * 3,
        in_specs=[SMEM] + [VMEM] * 10,
        out_specs=(ANY, ANY, VMEM),
        scratch_shapes=[
            pltpu.VMEM((E_ROWS, LANES), jnp.float32),
            pltpu.VMEM((E_ROWS, LANES), jnp.float32),
            pltpu.VMEM((CAP, LANES), jnp.float32),
            pltpu.VMEM((CAP, LANES), jnp.float32),
            pltpu.SemaphoreType.DMA((2, CAP // CHUNK)),
        ],
        compiler_params=params(),
        cost_estimate=cost(7 * CAP * LANES * 4),
        name="moments",
    )(offsets, *pinned(pieces + [fixes]), gradient)


def weights_kernel(turn, offsets, *refs):
    ratio, weight_out, held, buf, sems = refs[4:]
    begin, length = window(offsets)
    load_pieces(refs[:4], turn, held)

    def compute(row):
        master = held[pl.ds(begin + row, TILE), :]
        return (master - learn_rate * (ratio[pl.ds(row, TILE), :] + weight_decay * master),)

    chunked(length, compute, (weight_out,), (buf,), sems)


def weights(turn, offsets, pieces, ratio):
    return pl.pallas_call(
        functools.partial(weights_kernel, turn),
        out_shape=jax.ShapeDtypeStruct((CAP, LANES), jnp.float32),
        in_specs=[SMEM] + [VMEM] * 5,
        out_specs=ANY,
        scratch_shapes=[
            pltpu.VMEM((E_ROWS, LANES), jnp.float32),
            pltpu.VMEM((CAP, LANES), jnp.float32),
            pltpu.SemaphoreType.DMA((1, CAP // CHUNK)),
        ],
        compiler_params=params(),
        cost_estimate=cost(3 * CAP * LANES * 4),
        name="weights",
    )(offsets, *pinned(pieces + [ratio]))


def routes():
    ranks = range(OLD_RANKS)
    above = [(r + 1) % OLD_RANKS for r in ranks]
    own = [(2 * r, 2 * above[r]) for r in ranks] + [(2 * above[r] + 1, 2 * r + 1) for r in ranks]
    other = [(2 * r + 1, 2 * above[r]) for r in ranks] + [(2 * above[r], 2 * r + 1) for r in ranks]
    swap = [(i, i ^ 1) for i in range(N_DP)]
    return own, other, swap


def shards(
    old_weight,
    old_first,
    old_second,
    gradient,
    old_offsets,
    new_offsets,
    old_heads,
    new_heads,
    step_count,
):
    state = tuple(
        pltpu.with_memory_space_constraint(member[0, 0], pltpu.HBM)
        for member in (old_weight, old_first, old_second)
    )
    own_route, other_route, swap_route = routes()
    shift = [[(i, (i + s) % COLUMNS) for i in range(COLUMNS)] for s in range(COLUMNS)]

    def halos(groups):
        return [tuple((m, kind) for m in g) for g in groups for kind in ("own", "other")]

    swap_plan = [tuple((m, "swap") for m in ORDER)]
    plan = (swap_plan if SWAP_FIRST else []) + halos(GROUPS[:1])
    rest = ([] if SWAP_FIRST else swap_plan) + halos(GROUPS[1:])
    rest += [tuple((m, "keep") for m in g) for g in GROUPS]
    far_offsets = pltpu.with_memory_space_constraint(old_offsets, pltpu.HBM)
    *near, fixes = cut(far_offsets, state, plan, FIRST_LIMIT, step_count.reshape(1))
    near[0], later_offsets, old_heads = lax.optimization_barrier((near[0], old_offsets, old_heads))
    send, recv = tables(old_heads, new_heads)
    far = list(cut(later_offsets, state, rest, LIMIT))
    swapped = lax.ppermute((near if SWAP_FIRST else far).pop(0), "dp", swap_route)
    halves = near + far
    moved = [
        (
            lax.ppermute(halves[2 * g], "dp", own_route),
            lax.ppermute(halves[2 * g + 1], "dp", other_route),
        )
        for g in range(len(GROUPS))
    ]
    kept = halves[2 * len(GROUPS) :]
    pieces, turns = {}, {}
    for g, members in enumerate(GROUPS):
        turn = ORDER.index(members[0])
        parts = spread(turn, old_offsets, send, kept[g], moved[g][0], swapped, moved[g][1])
        parts = [parts[0]] + [lax.ppermute(parts[k], "tensor", shift[k]) for k in (1, 2, 3)]
        outer, inner = collect(recv, parts)
        arrived = [
            lax.ppermute(outer, "dp", other_route),
            outer,
            inner,
            lax.ppermute(inner, "dp", swap_route),
        ]
        for turn, m in enumerate(members):
            pieces[m], turns[m] = arrived, turn
    first, second, ratio = moments(
        (turns[1], turns[2]), new_offsets, fixes, pieces[1] + pieces[2], gradient[0, 0]
    )
    weight = weights(turns[0], new_offsets, pieces[0], ratio)
    return tuple(out[None, None] for out in (weight, first, second))


def solution(mesh):
    spread_out = P("dp", "tensor", None, None)
    return jax.shard_map(
        shards,
        mesh=mesh,
        in_specs=(spread_out,) * 4 + (P(),) * 5,
        out_specs=(spread_out,) * 3,
        check_vma=False,
    )
```
